32 devices in a mesh: groups: 1, expert: 16 (over z, y, x), tensor: 2 (over core).
Axes of the slice: x: 2, y: 2, z: 4, core: 2. Of those that a mesh axis runs over, the one named last changes fastest.
Arguments:
- tokens: bfloat16 [1024, 3584], P(('groups', 'expert'), 'tensor'), may hold values from -6 to 6
- expert_ids: int32 [1024, 8], P(('groups', 'expert')), may hold values from 0 to 15, all different within a row; in each aligned block of 64 rows (0 to 63, 64 to 127, ...) at most 36 rows name the same one
- route_weights: float32 [1024, 8], P(('groups', 'expert')), may hold values from 0.05 to 0.5
- gate_q: bfloat16 [16, 3584, 1024], P('expert', 'tensor'), may hold values from -4 to 4
- up_q: bfloat16 [16, 3584, 1024], P('expert', 'tensor'), may hold values from -4 to 4
- down_q: bfloat16 [16, 1024, 3584], P('expert', None, 'tensor'), may hold values from -4 to 4
- gate_scale: float32 [16, 28, 8], P('expert', 'tensor'), may hold values from 0.008351914 to 0.033407655
- up_scale: float32 [16, 28, 8], P('expert', 'tensor'), may hold values from 0.008351914 to 0.033407655
- down_scale: float32 [16, 8, 28], P('expert', None, 'tensor'), may hold values from 0.015625 to 0.0625
Outputs:
- mixed: bfloat16 [1024, 3584], P(('groups', 'expert'), 'tensor')
The draws below stay inside these ranges and needn't reach their ends.
Inputs may be any that keep to these rules, and one draw needn't show every extreme that they name: `expert_ids`: within the 64 token rows of one index of expert, no expert is named by more than 36 rows, a bound that some block reaches; a row names 8 different experts.
All inputs are finite; a program needn't handle non-finite values.
Results may differ from the reference program's by a relative error of at most 0.0076.
Values may be sent and summed in bfloat16 or wider, within the bound.
A program may use at most 128 MiB of HBM per device.

```python
import math
import jax
import jax.numpy as jnp
import numpy as np
from jax import lax

D = 3584
FF = 1024
TOP = 8
TOK_DEV = 64
EXPERTS = 16
SPLIT = 1
CAP = 36
TOKENS = 1024
N_EXPERT = 16


def levels(own_key, shape, shards, smallest, high):
    gain = 1.0
    for axis_at, blocks in shards:
        draws = jax.random.uniform(jax.random.fold_in(jax.random.fold_in(own_key, 6), axis_at), (blocks,), jnp.float32, smallest / len(shards), high / len(shards))
        gain = gain * jnp.repeat(jnp.exp(draws), shape[axis_at] // blocks).reshape((-1,) + (1,) * (len(shape) - 1 - axis_at))
    return gain


def assign_block(stream_key, own, number, rows, number_of, top, reach, lean):
    ranking = jax.random.permutation(stream_key, number_of)
    crowded, ordinary = shares(number_of, rows * top, reach, lean, True), shares(number_of, rows * top, reach, lean, False)
    places = jnp.arange(number_of)

    def named(lengths, turn):
        used = int((lengths > 0).sum())
        fixed = max(1, used // 4)
        moved = fixed + (places - fixed + turn * (used - fixed)) % max(1, number_of - fixed)
        return jnp.zeros((number_of,), jnp.int32).at[ranking[jnp.where(places < fixed, places, moved)]].set(jnp.asarray(lengths, jnp.int32))

    lengths = jnp.where(number % 4 == 0, named(crowded, number // 4), named(ordinary, number - number // 4 - 1))
    mixed = jax.random.permutation(jax.random.fold_in(own, 3), number_of)
    donor, sink = mixed[0:number_of // 2 * 2:2], mixed[1:number_of // 2 * 2:2]
    room = jnp.minimum(lengths[donor] - 1, reach - lengths[sink]) // 2
    room = jnp.where((donor == ranking[0]) | (sink == ranking[0]) | (lengths[sink] == 0), 0, jnp.maximum(room, 0))
    moved = jax.random.randint(jax.random.fold_in(own, 4), (number_of // 2,), 0, 1 << 20) % (room + 1)
    lengths = lengths.at[donor].add(-moved).at[sink].add(moved)
    members = jnp.searchsorted(jnp.cumsum(lengths), jnp.arange(rows * top), side="right").astype(jnp.int32)
    grid = members.reshape(top, rows).T
    grid = grid[jax.random.permutation(jax.random.fold_in(own, 1), rows)]
    turn = jax.random.randint(jax.random.fold_in(own, 2), (rows, 1), 0, top)
    return jnp.take_along_axis(grid, (jnp.arange(top)[None, :] + turn) % top, axis=1)


def shares(number_of, total, reach, slope, full):
    portions = [(1 << 20) // math.isqrt(grade ** slope) + 1 for grade in range(1, number_of + 1)]
    largest = reach if full else min(reach, max(-(-total // number_of), total * portions[0] // sum(portions)))
    least = 1 if total - largest >= number_of - 1 else 0
    holding, surplus = [largest] + [least] * (number_of - 1), total - largest - least * (number_of - 1)
    while surplus > 0:
        free = [i for i in range(1, number_of) if holding[i] < largest] or [i for i in range(1, number_of) if holding[i] < reach]
        pool, remaining = sum([portions[i] for i in free]), surplus
        for i in free:
            addition = min(reach - holding[i], max(1, remaining * portions[i] // pool), surplus)
            holding[i] = holding[i] + addition
            surplus = surplus - addition
    return np.array(holding)


def centred(stream_key, shape, width, bound, shards=(), kind=jnp.bfloat16):
    entries = jax.random.normal(stream_key, shape, jnp.float32) * width
    if len(shards) > 0:
        entries = levels(stream_key, shape, shards, -0.22, 0.18) * entries
    return jnp.clip(entries, min=-bound, max=bound).astype(kind)


def setup_inputs(seed: int = 0, part: int = 0) -> dict:
    keys = jax.random.split(jax.random.key(seed), 10)
    part_keys = jax.random.split(jax.random.fold_in(keys[9], part), 10)
    tokens = centred(part_keys[0], (TOKENS, D), 1.0, 6.0, ((0, 16), (1, 2)))
    expert_ids_keys = jax.random.split(jax.random.fold_in(part_keys[1], 1), TOKENS // TOK_DEV)
    expert_ids_turns = jax.random.permutation(jax.random.fold_in(part_keys[1], 3), TOKENS // TOK_DEV)
    expert_ids = jax.vmap(lambda own, number: assign_block(jax.random.fold_in(part_keys[1], 2), own, number, TOK_DEV, EXPERTS, TOP, CAP, 1))(expert_ids_keys, expert_ids_turns).reshape((TOKENS, TOP))
    route_weights = jnp.clip(jnp.exp(math.log(0.5) - 2.3025851 * jax.random.uniform(part_keys[2], (TOKENS, TOP), jnp.float32) ** levels(part_keys[2], (TOKENS, TOP), ((0, 16),), -0.2, 0.2)), 0.05, 0.5)
    gate_q = centred(keys[3], (EXPERTS * SPLIT, D, FF // SPLIT), 1.0, 4.0, ((0, 16), (1, 2)))
    up_q = centred(keys[4], (EXPERTS * SPLIT, D, FF // SPLIT), 1.0, 4.0, ((0, 16), (1, 2)))
    down_q = centred(keys[5], (EXPERTS * SPLIT, FF // SPLIT, D), 1.0, 4.0, ((0, 16), (2, 2)))
    gate_scale = jnp.clip(jnp.exp(math.log(0.033407655) - 1.3862944 * jax.random.uniform(keys[6], (EXPERTS * SPLIT, D // 128, FF // SPLIT // 128), jnp.float32) ** levels(keys[6], (EXPERTS * SPLIT, D // 128, FF // SPLIT // 128), ((0, 16), (1, 2)), -0.2, 0.2)), 0.008351914, 0.033407655)
    up_scale = jnp.clip(jnp.exp(math.log(0.033407655) - 1.3862944 * jax.random.uniform(keys[7], (EXPERTS * SPLIT, D // 128, FF // SPLIT // 128), jnp.float32) ** levels(keys[7], (EXPERTS * SPLIT, D // 128, FF // SPLIT // 128), ((0, 16), (1, 2)), -0.2, 0.2)), 0.008351914, 0.033407655)
    down_scale = jnp.clip(jnp.exp(math.log(0.0625) - 1.3862944 * jax.random.uniform(keys[8], (EXPERTS * SPLIT, FF // SPLIT // 128, D // 128), jnp.float32) ** levels(keys[8], (EXPERTS * SPLIT, FF // SPLIT // 128, D // 128), ((0, 16), (2, 2)), -0.2, 0.2)), 0.015625, 0.0625)
    return dict(tokens=tokens, expert_ids=expert_ids, route_weights=route_weights, gate_q=gate_q, up_q=up_q, down_q=down_q, gate_scale=gate_scale, up_scale=up_scale, down_scale=down_scale)


def dequant(quant, scales):
    height, breadth = quant.shape
    blocks = quant.reshape(height // 128, 128, breadth // 128, 128).astype(jnp.float32) * scales[:, None, :, None]
    return blocks.reshape(height, breadth).astype(jnp.bfloat16)


def part_apply(gathered, w_gate, w_up, w_down):
    gate = jnp.dot(gathered, w_gate, preferred_element_type=jnp.float32)
    upward = jnp.dot(gathered, w_up, preferred_element_type=jnp.float32)
    hidden = (jax.nn.silu(gate) * upward).astype(jnp.bfloat16)
    return jnp.dot(hidden, w_down, preferred_element_type=jnp.float32).astype(jnp.bfloat16)


def reference(tokens, expert_ids, route_weights, gate_q, up_q, down_q, gate_scale, up_scale, down_scale):
    flat_ids = expert_ids.reshape(-1)
    flat_weights = route_weights.reshape(-1)
    capacity_all = N_EXPERT * CAP

    def per_expert(routed, expert):
        matches = flat_ids == expert
        chosen = jnp.nonzero(matches, size=capacity_all, fill_value=0)[0].astype(jnp.int32)
        occupied = (jnp.arange(capacity_all) < jnp.sum(matches.astype(jnp.int32))).astype(jnp.float32)
        holders = (chosen // TOP).astype(jnp.int32)
        gathered = tokens[holders]
        total = jnp.zeros((capacity_all, D), jnp.float32)
        for part in range(SPLIT):
            entry = expert * SPLIT + part
            result = part_apply(gathered, dequant(gate_q[entry], gate_scale[entry]), dequant(up_q[entry], up_scale[entry]), dequant(down_q[entry], down_scale[entry]))
            total = total + result.astype(jnp.float32)
        rounded = lax.optimization_barrier(total.astype(jnp.bfloat16)).astype(jnp.float32)
        scaled = rounded * (flat_weights[chosen] * occupied)[:, None]
        return routed.at[holders].add(scaled), None

    routed, _ = lax.scan(per_expert, jnp.zeros((TOKENS, D), jnp.float32), jnp.arange(EXPERTS, dtype=jnp.int32))
    return routed.astype(jnp.bfloat16)
```

```python
import jax
import jax.numpy as jnp
from jax import lax
from jax.experimental import pallas as pl
from jax.experimental.pallas import tpu as pltpu
from jax.sharding import PartitionSpec as P

FF = 1024


def dequant(quant, scales):
    height, breadth = quant.shape
    blocks = (
        quant.reshape(height // 128, 128, breadth // 128, 128).astype(jnp.float32)
        * scales[:, None, :, None]
    )
    return blocks.reshape(height, breadth).astype(jnp.bfloat16)


def exchange_local(
    tokens, expert_ids, route_weights, gate_q, up_q, down_q, gate_scale, up_scale, down_scale
):
    holders = lax.axis_size("expert")
    tok_rows, half_width = tokens.shape
    pick_count = expert_ids.shape[1]
    slices = FF // gate_q.shape[2]
    experts = holders // slices
    capacity = max(
        2, min(tok_rows, tok_rows * pick_count // experts + tok_rows * pick_count // (8 * experts))
    )
    slot_range = experts * capacity
    flat_ids = expert_ids.reshape(-1)
    onehot = (flat_ids[:, None] == jnp.arange(experts)[None, :]).astype(jnp.int32)
    before = jnp.cumsum(onehot, axis=0) - onehot
    position = jnp.sum(before * onehot, axis=1)
    slot_ids = flat_ids * capacity + position
    placing = (slot_ids[:, None] == jnp.arange(slot_range)[None, :]).astype(jnp.int32)
    pair_owner = jnp.arange(tok_rows * pick_count, dtype=jnp.int32) // pick_count
    token_of_slot = jnp.sum(placing * pair_owner[:, None], axis=0)
    occupied = jnp.sum(placing, axis=0) > 0
    filled = jnp.where(occupied[:, None], tokens[token_of_slot], jnp.zeros((), jnp.bfloat16))
    w_gate = dequant(gate_q[0], gate_scale[0])
    w_up = dequant(up_q[0], up_scale[0])
    w_down = dequant(down_q[0], down_scale[0])
    ff_width = w_gate.shape[1]
    outgoing = jnp.repeat(filled.reshape(experts, capacity, half_width), slices, axis=0)
    received = lax.all_to_all(outgoing, "expert", split_axis=0, concat_axis=0, tiled=True)
    sources, slots_here, _ = received.shape
    row_block = received.reshape(sources * slots_here, half_width)
    partial_value = jnp.concatenate(
        [
            jnp.dot(row_block, w_gate, preferred_element_type=jnp.float32),
            jnp.dot(row_block, w_up, preferred_element_type=jnp.float32),
        ],
        axis=1,
    )
    summed = lax.psum(partial_value, "tensor")
    hidden = (jax.nn.silu(summed[:, :ff_width]) * summed[:, ff_width:]).astype(jnp.bfloat16)
    term = jnp.dot(hidden, w_down, preferred_element_type=jnp.float32)
    result = term.astype(jnp.bfloat16).astype(jnp.float32)
    result = result.astype(jnp.bfloat16)
    returned = lax.all_to_all(
        result.reshape(sources, slots_here, half_width),
        "expert",
        split_axis=0,
        concat_axis=0,
        tiled=True,
    )
    combined = jnp.sum(
        returned.reshape(experts, slices, capacity, half_width).astype(jnp.float32), axis=1
    )
    rounded = lax.optimization_barrier(combined.astype(jnp.bfloat16)).astype(jnp.float32)
    flat_back = rounded.reshape(slot_range, half_width)
    picked = flat_back[slot_ids].reshape(tok_rows, pick_count, half_width)
    routed = jnp.zeros((tok_rows, half_width), jnp.float32)
    for column in range(pick_count):
        routed = routed + route_weights[:, column : column + 1] * picked[:, column]
    return routed.astype(jnp.bfloat16)


MESH = pl.DeviceIdType.MESH
ROWS = 64


def peer(e, d):
    out = e
    for bit in (1, 2, 4, 8):
        if d & bit:
            out = out + bit - 2 * bit * ((e // bit) % 2)
    return out


def fused_kernel(
    tok_ref, ids_ref, rw_ref, gs_ref, us_ref, ds_ref, gate_hbm, up_hbm, down_hbm, out_ref,
    tok, w_in, w_down, scale_in, scale_down, part_own, part_out, part_in, hid, part_y,
    diag_in, near_in, far_in, col_out, z_in, wrow_out, wrow_in,
    load_sem, tok_send, tok_recv, part_send, part_recv, row_send, row_recv,
    y_send, y_recv, z_send, z_recv,
):
    e = lax.axis_index("expert")
    c = lax.axis_index("tensor")
    half = tok_ref.shape[1]
    ff = w_down.shape[0]
    loads = [
        pltpu.make_async_copy(gate_hbm.at[0], w_in.at[0], load_sem.at[0]),
        pltpu.make_async_copy(up_hbm.at[0], w_in.at[1], load_sem.at[1]),
        pltpu.make_async_copy(down_hbm.at[0], w_down, load_sem.at[2]),
    ]
    for load in loads:
        load.start()

    barrier = pltpu.get_barrier_semaphore()
    for d in range(1, 16):
        pl.semaphore_signal(barrier, inc=1, device_id={"expert": peer(e, d)}, device_id_type=MESH)
    pl.semaphore_signal(barrier, inc=1, device_id={"tensor": 1 - c}, device_id_type=MESH)

    eye = lax.broadcasted_iota(jnp.int32, (ROWS, ROWS), 0) == lax.broadcasted_iota(
        jnp.int32, (ROWS, ROWS), 1
    )
    ids = ids_ref[...]
    rw = rw_ref[...]
    for d in range(16):
        column = jnp.sum(jnp.where(ids == peer(e, d), rw, 0.0), axis=1, keepdims=True)
        row = jnp.sum(jnp.where(eye, column, 0.0), axis=0, keepdims=True)
        wrow_out[d, :, 0:ROWS] = jnp.broadcast_to(row, (8, ROWS))
    tok[0, 0] = tok_ref[...]
    pl.semaphore_wait(barrier, 16)

    def send(src, dst, s_sem, r_sem, **where):
        return pltpu.make_async_remote_copy(
            src_ref=src, dst_ref=dst, send_sem=s_sem, recv_sem=r_sem,
            device_id=where, device_id_type=MESH,
        )

    tok_z = [
        send(tok_ref, tok.at[0, dz], tok_send.at[0, dz], tok_recv.at[0, dz], expert=peer(e, 4 * dz))
        for dz in range(1, 4)
    ]
    tok_xy = [
        [
            send(
                tok.at[0, dz] if dz else tok_ref, tok.at[k, dz], tok_send.at[k, dz],
                tok_recv.at[k, dz], expert=peer(e, k),
            )
            for k in (1, 2)
        ]
        for dz in range(4)
    ]
    near = 1 + c
    far = 2 - c
    near_dev = e + (1 - c) * (1 - 2 * (e % 2)) + c * (2 - 4 * ((e // 2) % 2))
    far_dev = e + c * (1 - 2 * (e % 2)) + (1 - c) * (2 - 4 * ((e // 2) % 2))
    tok_diag = [
        send(tok.at[near, dz], tok.at[3, dz], tok_send.at[3, dz], tok_recv.at[3, dz], expert=far_dev)
        for dz in range(4)
    ]

    def wait_tok(k, dz):
        send(tok.at[k, dz], tok.at[k, dz], tok_send.at[0, 0], tok_recv.at[k, dz], expert=near_dev).wait_recv()

    for cp in tok_xy[0]:
        cp.start()
    for cp in tok_z:
        cp.start()
    rows_sent = [
        send(wrow_out.at[d], wrow_in.at[d], row_send.at[d], row_recv.at[d], expert=peer(e, d))
        for d in range(1, 16)
    ]
    for cp in rows_sent:
        cp.start()

    wrow_in[0] = wrow_out[0]
    for g, ref in ((0, gs_ref), (1, us_ref)):
        blocks = ref[0]
        for j in range(ff // 128):
            scale_in[g, 0 : half // 128, j * 128 : (j + 1) * 128] = jnp.broadcast_to(
                blocks[:, j : j + 1], (half // 128, 128)
            )
    blocks = ds_ref[0]
    for j in range(half // 128):
        scale_down[:, j * 128 : (j + 1) * 128] = jnp.broadcast_to(blocks[:, j : j + 1], (ff // 128, 128))

    def dequant_in(g):
        loads[g].wait()

        @pl.loop(0, half // 128)
        def _(i):
            at = pl.ds(pl.multiple_of(i * 128, 128), 128)
            w_in[g, at, :] = (w_in[g, at, :].astype(jnp.float32) * scale_in[g, pl.ds(i, 1), :]).astype(jnp.bfloat16)

    def dequant_down():
        loads[2].wait()

        @pl.loop(0, ff // 128)
        def _(i):
            at = pl.ds(pl.multiple_of(i * 128, 128), 128)
            w_down[at, :] = (w_down[at, :].astype(jnp.float32) * scale_down[pl.ds(i, 1), :]).astype(jnp.bfloat16)

    def pass_on(dz):
        tok_z[dz - 1].wait_recv()
        for cp in tok_xy[dz]:
            cp.start()

    def pass_diag(dz):
        wait_tok(near, dz)
        tok_diag[dz].start()

    parts = [
        send(part_out.at[k], part_in.at[k], part_send.at[k], part_recv.at[k], tensor=1 - c)
        for k in range(4)
    ]

    def gate_up(k):
        x = tok[k].reshape(4 * ROWS, half)

        @pl.loop(0, 2 * ff // 256)
        def _(t):
            g = t // (ff // 256)
            at = pl.ds(pl.multiple_of((t % (ff // 256)) * 256, 256), 256)
            p = jnp.dot(x, w_in[g, :, at], preferred_element_type=jnp.float32)
            part_own[k % 2, g, :, at] = p
            part_out[k, g, :, at] = p.astype(jnp.bfloat16)

        parts[k].start()

    def down(k):
        parts[k].wait_recv()

        @pl.loop(0, ff // 256)
        def _(t):
            at = pl.ds(pl.multiple_of(t * 256, 256), 256)
            gate = part_own[k % 2, 0, :, at] + part_in[k, 0, :, at].astype(jnp.float32)
            up = part_own[k % 2, 1, :, at] + part_in[k, 1, :, at].astype(jnp.float32)
            hid[:, at] = (gate / (1.0 + jnp.exp(-gate)) * up).astype(jnp.bfloat16)

        columns = []
        for dz in range(4):
            row = wrow_in[4 * dz + k, 0:1, 0:ROWS]
            columns.append(jnp.sum(jnp.where(eye, row, 0.0), axis=1, keepdims=True))
        column = jnp.concatenate(columns, axis=0)
        h = hid[...]

        @pl.loop(0, half // 256)
        def _(t):
            at = pl.ds(pl.multiple_of(t * 256, 256), 256)
            y = jnp.dot(h, w_down[:, at], preferred_element_type=jnp.float32) * column
            part_y[k, :, :, at] = y.reshape(4, ROWS, 256).astype(jnp.bfloat16)

    diag_back = [
        send(part_y.at[3, dz], diag_in.at[dz], y_send.at[0, dz], y_recv.at[0, dz], expert=near_dev)
        for dz in range(4)
    ]
    near_back = [
        send(part_y.at[near, dz], near_in.at[dz], y_send.at[1, dz], y_recv.at[1, dz], expert=near_dev)
        for dz in range(4)
    ]
    far_back = [
        send(part_y.at[far, dz], far_in.at[dz], y_send.at[2, dz], y_recv.at[2, dz], expert=far_dev)
        for dz in range(4)
    ]
    z_back = [
        send(col_out.at[dz], z_in.at[dz], z_send.at[dz], z_recv.at[dz], expert=peer(e, 4 * dz))
        for dz in range(1, 4)
    ]

    dequant_in(0)
    pass_diag(0)
    pass_on(1)
    dequant_in(1)
    pass_on(2)
    pass_diag(1)
    dequant_down()
    pass_on(3)
    for cp in rows_sent:
        cp.wait_recv()
    gate_up(0)
    pass_diag(2)
    down(0)
    pass_diag(3)
    for dz in range(4):
        wait_tok(far, dz)
    gate_up(1)
    gate_up(2)
    down(1)
    down(2)
    for cp in near_back:
        cp.start()
    for dz in range(4):
        tok_diag[dz].wait_recv()
    gate_up(3)
    down(3)
    for cp in diag_back:
        cp.start()
    order = (1, 2, 3, 0)
    for dz in order:
        diag_back[dz].wait_recv()
        part_y[far, dz] = (
            part_y[far, dz].astype(jnp.float32) + diag_in[dz].astype(jnp.float32)
        ).astype(jnp.bfloat16)
        far_back[dz].start()
    for dz in order:
        near_back[dz].wait_recv()
        far_back[dz].wait_recv()
        total = (
            part_y[0, dz].astype(jnp.float32)
            + near_in[dz].astype(jnp.float32)
            + far_in[dz].astype(jnp.float32)
        )
        if dz:
            col_out[dz] = total.astype(jnp.bfloat16)
            z_back[dz - 1].start()
    for dz in range(1, 4):
        z_back[dz - 1].wait_recv()
        total = total + z_in[dz].astype(jnp.float32)
    out_ref[...] = total.astype(jnp.bfloat16)

    for cp in (
        tok_z + rows_sent + parts + tok_diag + diag_back + near_back + far_back + z_back
        + [cp for pair in tok_xy for cp in pair]
    ):
        cp.wait_send()


def fused_local(
    tokens, expert_ids, route_weights, gate_q, up_q, down_q, gate_scale, up_scale, down_scale
):
    rows, half = tokens.shape
    ff = gate_q.shape[2]
    bf16, f32 = jnp.bfloat16, jnp.float32
    vmem = pl.BlockSpec(memory_space=pltpu.VMEM)
    hbm = pl.BlockSpec(memory_space=pl.ANY)
    dma = pltpu.SemaphoreType.DMA
    return pl.pallas_call(
        fused_kernel,
        out_shape=jax.ShapeDtypeStruct((rows, half), bf16),
        in_specs=[vmem] * 6 + [hbm] * 3,
        out_specs=vmem,
        scratch_shapes=[
            pltpu.VMEM((4, 4, rows, half), bf16),
            pltpu.VMEM((2, half, ff), bf16),
            pltpu.VMEM((ff, half), bf16),
            pltpu.VMEM((2, 16, ff), f32),
            pltpu.VMEM((ff // 128, half), f32),
            pltpu.VMEM((2, 2, 4 * rows, ff), f32),
            pltpu.VMEM((4, 2, 4 * rows, ff), bf16),
            pltpu.VMEM((4, 2, 4 * rows, ff), bf16),
            pltpu.VMEM((4 * rows, ff), bf16),
            pltpu.VMEM((4, 4, rows, half), bf16),
            pltpu.VMEM((4, rows, half), bf16),
            pltpu.VMEM((4, rows, half), bf16),
            pltpu.VMEM((4, rows, half), bf16),
            pltpu.VMEM((4, rows, half), bf16),
            pltpu.VMEM((4, rows, half), bf16),
            pltpu.VMEM((16, 8, 128), f32),
            pltpu.VMEM((16, 8, 128), f32),
            dma((3,)),
            dma((4, 4)),
            dma((4, 4)),
            dma((4,)),
            dma((4,)),
            dma((16,)),
            dma((16,)),
            dma((3, 4)),
            dma((3, 4)),
            dma((4,)),
            dma((4,)),
        ],
        compiler_params=pltpu.CompilerParams(
            collective_id=0, has_side_effects=True, vmem_limit_bytes=58 * 1024 * 1024
        ),
        cost_estimate=pl.CostEstimate(
            flops=2 * 16 * rows * half * ff * 3,
            bytes_accessed=3 * 2 * half * ff,
            transcendentals=16 * rows * ff,
        ),
    )(tokens, expert_ids, route_weights, gate_scale, up_scale, down_scale, gate_q, up_q, down_q)


def solution(mesh):
    return jax.shard_map(
        fused_local if mesh.shape["expert"] == 16 and mesh.shape["tensor"] == 2 else exchange_local,
        mesh=mesh,
        in_specs=(
            P(("groups", "expert"), "tensor"),
            P(("groups", "expert"), None),
            P(("groups", "expert"), None),
            P("expert", "tensor", None),
            P("expert", "tensor", None),
            P("expert", None, "tensor"),
            P("expert", "tensor", None),
            P("expert", "tensor", None),
            P("expert", None, "tensor"),
        ),
        out_specs=P(("groups", "expert"), "tensor"),
        check_vma=False,
    )
```

```python
import jax
import jax.numpy as jnp
from jax import lax
from jax.experimental import pallas as pl
from jax.experimental.pallas import tpu as pltpu
from jax.sharding import PartitionSpec as P

FF = 1024


def dequant(quant, scales):
    height, breadth = quant.shape
    blocks = (
        quant.reshape(height // 128, 128, breadth // 128, 128).astype(jnp.float32)
        * scales[:, None, :, None]
    )
    return blocks.reshape(height, breadth).astype(jnp.bfloat16)


def exchange_local(
    tokens, expert_ids, route_weights, gate_q, up_q, down_q, gate_scale, up_scale, down_scale
):
    holders = lax.axis_size("expert")
    tok_rows, half_width = tokens.shape
    pick_count = expert_ids.shape[1]
    slices = FF // gate_q.shape[2]
    experts = holders // slices
    capacity = max(
        2, min(tok_rows, tok_rows * pick_count // experts + tok_rows * pick_count // (8 * experts))
    )
    slot_range = experts * capacity
    flat_ids = expert_ids.reshape(-1)
    onehot = (flat_ids[:, None] == jnp.arange(experts)[None, :]).astype(jnp.int32)
    before = jnp.cumsum(onehot, axis=0) - onehot
    position = jnp.sum(before * onehot, axis=1)
    slot_ids = flat_ids * capacity + position
    placing = (slot_ids[:, None] == jnp.arange(slot_range)[None, :]).astype(jnp.int32)
    pair_owner = jnp.arange(tok_rows * pick_count, dtype=jnp.int32) // pick_count
    token_of_slot = jnp.sum(placing * pair_owner[:, None], axis=0)
    occupied = jnp.sum(placing, axis=0) > 0
    filled = jnp.where(occupied[:, None], tokens[token_of_slot], jnp.zeros((), jnp.bfloat16))
    w_gate = dequant(gate_q[0], gate_scale[0])
    w_up = dequant(up_q[0], up_scale[0])
    w_down = dequant(down_q[0], down_scale[0])
    ff_width = w_gate.shape[1]
    outgoing = jnp.repeat(filled.reshape(experts, capacity, half_width), slices, axis=0)
    received = lax.all_to_all(outgoing, "expert", split_axis=0, concat_axis=0, tiled=True)
    sources, slots_here, _ = received.shape
    row_block = received.reshape(sources * slots_here, half_width)
    partial_value = jnp.concatenate(
        [
            jnp.dot(row_block, w_gate, preferred_element_type=jnp.float32),
            jnp.dot(row_block, w_up, preferred_element_type=jnp.float32),
        ],
        axis=1,
    )
    summed = lax.psum(partial_value, "tensor")
    hidden = (jax.nn.silu(summed[:, :ff_width]) * summed[:, ff_width:]).astype(jnp.bfloat16)
    term = jnp.dot(hidden, w_down, preferred_element_type=jnp.float32)
    result = term.astype(jnp.bfloat16).astype(jnp.float32)
    result = result.astype(jnp.bfloat16)
    returned = lax.all_to_all(
        result.reshape(sources, slots_here, half_width),
        "expert",
        split_axis=0,
        concat_axis=0,
        tiled=True,
    )
    combined = jnp.sum(
        returned.reshape(experts, slices, capacity, half_width).astype(jnp.float32), axis=1
    )
    rounded = lax.optimization_barrier(combined.astype(jnp.bfloat16)).astype(jnp.float32)
    flat_back = rounded.reshape(slot_range, half_width)
    picked = flat_back[slot_ids].reshape(tok_rows, pick_count, half_width)
    routed = jnp.zeros((tok_rows, half_width), jnp.float32)
    for column in range(pick_count):
        routed = routed + route_weights[:, column : column + 1] * picked[:, column]
    return routed.astype(jnp.bfloat16)


MESH = pl.DeviceIdType.MESH
ROWS = 64


def peer(e, d):
    out = e
    for bit in (1, 2, 4, 8):
        if d & bit:
            out = out + bit - 2 * bit * ((e // bit) % 2)
    return out


def fused_kernel(
    tok_ref, ids_ref, rw_ref, gs_ref, us_ref, ds_ref, gate_hbm, up_hbm, down_hbm, out_ref,
    tok, w_in, w_down, scale_in, scale_down, part_own, part_out, part_in, hid, part_y,
    diag_in, near_in, far_in, col_out, z_in, acc, wrow_out, wrow_in,
    load_sem, tok_send, tok_recv, part_send, part_recv, row_send, row_recv,
    y_send, y_recv, z_send, z_recv,
):
    e = lax.axis_index("expert")
    c = lax.axis_index("tensor")
    half = tok_ref.shape[1]
    ff = w_down.shape[0]
    loads = [
        pltpu.make_async_copy(gate_hbm.at[0], w_in.at[0], load_sem.at[0]),
        pltpu.make_async_copy(up_hbm.at[0], w_in.at[1], load_sem.at[1]),
        pltpu.make_async_copy(down_hbm.at[0], w_down, load_sem.at[2]),
    ]
    for load in loads:
        load.start()

    barrier = pltpu.get_barrier_semaphore()
    for d in range(1, 16):
        pl.semaphore_signal(barrier, inc=1, device_id={"expert": peer(e, d)}, device_id_type=MESH)
    pl.semaphore_signal(barrier, inc=1, device_id={"tensor": 1 - c}, device_id_type=MESH)

    eye = lax.broadcasted_iota(jnp.int32, (ROWS, ROWS), 0) == lax.broadcasted_iota(
        jnp.int32, (ROWS, ROWS), 1
    )
    ids = ids_ref[...]
    rw = rw_ref[...]
    for d in range(16):
        row = jnp.sum(jnp.where(ids == peer(e, d), rw, 0.0), axis=0, keepdims=True)
        wrow_out[d, :, 0:ROWS] = jnp.broadcast_to(row, (8, ROWS))
    tok[0, 0] = tok_ref[...]
    pl.semaphore_wait(barrier, 16)

    def send(src, dst, s_sem, r_sem, **where):
        return pltpu.make_async_remote_copy(
            src_ref=src, dst_ref=dst, send_sem=s_sem, recv_sem=r_sem,
            device_id=where, device_id_type=MESH,
        )

    tok_z = [
        send(tok_ref, tok.at[dz, 0], tok_send.at[dz, 0], tok_recv.at[dz, 0], expert=peer(e, 4 * dz))
        for dz in range(1, 4)
    ]
    tok_xy = [
        [
            send(
                tok.at[dz, 0] if dz else tok_ref, tok.at[dz, k], tok_send.at[dz, k],
                tok_recv.at[dz, k], expert=peer(e, k),
            )
            for k in (1, 2)
        ]
        for dz in range(4)
    ]
    near = 1 + c
    far = 2 - c
    near_dev = e + (1 - c) * (1 - 2 * (e % 2)) + c * (2 - 4 * ((e // 2) % 2))
    far_dev = e + c * (1 - 2 * (e % 2)) + (1 - c) * (2 - 4 * ((e // 2) % 2))
    tok_diag = [
        send(tok.at[dz, near], tok.at[dz, 3], tok_send.at[dz, 3], tok_recv.at[dz, 3], expert=far_dev)
        for dz in range(4)
    ]

    def wait_tok(k, dz):
        send(tok.at[dz, k], tok.at[dz, k], tok_send.at[0, 0], tok_recv.at[dz, k], expert=near_dev).wait_recv()

    for cp in tok_xy[0]:
        cp.start()
    for cp in tok_z:
        cp.start()
    rows_sent = [
        send(wrow_out.at[d], wrow_in.at[d], row_send.at[d], row_recv.at[d], expert=peer(e, d))
        for d in range(1, 16)
    ]
    for cp in rows_sent:
        cp.start()

    wrow_in[0] = wrow_out[0]
    square = (half // 128, half // 128)
    diagonal = lax.broadcasted_iota(jnp.int32, square, 0) == lax.broadcasted_iota(jnp.int32, square, 1)
    for g, ref in ((0, gs_ref), (1, us_ref)):
        blocks = ref[0]
        for j in range(ff // 128):
            row = blocks[j : j + 1, :]
            column = jnp.sum(jnp.where(diagonal, row, 0.0), axis=1, keepdims=True)
            scale_in[g, 0 : half // 128, j * 128 : (j + 1) * 128] = jnp.broadcast_to(
                column, (half // 128, 128)
            )
    blocks = ds_ref[0]
    for j in range(half // 128):
        scale_down[:, j * 128 : (j + 1) * 128] = jnp.broadcast_to(blocks[:, j : j + 1], (ff // 128, 128))

    def dequant_in(g):
        loads[g].wait()

        @pl.loop(0, half // 128)
        def _(i):
            at = pl.ds(pl.multiple_of(i * 128, 128), 128)
            w_in[g, at, :] = (w_in[g, at, :].astype(jnp.float32) * scale_in[g, pl.ds(i, 1), :]).astype(jnp.bfloat16)

    def dequant_down():
        loads[2].wait()

        @pl.loop(0, ff // 128)
        def _(i):
            at = pl.ds(pl.multiple_of(i * 128, 128), 128)
            w_down[at, :] = (w_down[at, :].astype(jnp.float32) * scale_down[pl.ds(i, 1), :]).astype(jnp.bfloat16)

    def pass_on(dz):
        tok_z[dz - 1].wait_recv()
        for cp in tok_xy[dz]:
            cp.start()

    def pass_diag(dz):
        wait_tok(near, dz)
        tok_diag[dz].start()

    parts = [
        send(part_out.at[k], part_in.at[k], part_send.at[k], part_recv.at[k], tensor=1 - c)
        for k in range(4)
    ]

    def gate_up(k):
        wait_tok(far, k)
        tok_diag[k].wait_recv()
        x = tok[k].reshape(4 * ROWS, half)

        @pl.loop(0, 2 * ff // 256)
        def _(t):
            g = t // (ff // 256)
            at = pl.ds(pl.multiple_of((t % (ff // 256)) * 256, 256), 256)
            p = jnp.dot(x, w_in[g, :, at], preferred_element_type=jnp.float32)
            part_own[k % 2, g, :, at] = p
            part_out[k, g, :, at] = p.astype(jnp.bfloat16)

        parts[k].start()

    def down(k):
        parts[k].wait_recv()

        @pl.loop(0, ff // 256)
        def _(t):
            at = pl.ds(pl.multiple_of(t * 256, 256), 256)
            gate = part_own[k % 2, 0, :, at] + part_in[k, 0, :, at].astype(jnp.float32)
            up = part_own[k % 2, 1, :, at] + part_in[k, 1, :, at].astype(jnp.float32)
            hid[:, at] = (gate / (1.0 + jnp.exp(-gate)) * up).astype(jnp.bfloat16)

        columns = []
        for d in range(4):
            row = wrow_in[4 * k + d, 0:1, 0:ROWS]
            columns.append(jnp.sum(jnp.where(eye, row, 0.0), axis=1, keepdims=True))
        column = jnp.concatenate(columns, axis=0)
        h = hid[...]

        @pl.loop(0, half // 256)
        def _(t):
            at = pl.ds(pl.multiple_of(t * 256, 256), 256)
            y = jnp.dot(h, w_down[:, at], preferred_element_type=jnp.float32) * column
            part_y[k, :, :, at] = y.reshape(4, ROWS, 256).astype(jnp.bfloat16)

    diag_back = [
        send(part_y.at[dz, 3], diag_in.at[dz], y_send.at[0, dz], y_recv.at[0, dz], expert=near_dev)
        for dz in range(4)
    ]
    near_back = [
        send(part_y.at[dz, near], near_in.at[dz], y_send.at[1, dz], y_recv.at[1, dz], expert=near_dev)
        for dz in range(4)
    ]
    far_back = [
        send(part_y.at[dz, far], far_in.at[dz], y_send.at[2, dz], y_recv.at[2, dz], expert=far_dev)
        for dz in range(4)
    ]
    z_back = [
        send(col_out.at[dz], z_in.at[dz], z_send.at[dz], z_recv.at[dz], expert=peer(e, 4 * dz))
        for dz in range(1, 4)
    ]

    def back(dz):
        near_back[dz].start()
        diag_back[dz].start()

    def turn(dz):
        diag_back[dz].wait_recv()
        part_y[dz, far] = (
            part_y[dz, far].astype(jnp.float32) + diag_in[dz].astype(jnp.float32)
        ).astype(jnp.bfloat16)
        far_back[dz].start()

    def column_sum(dz):
        near_back[dz].wait_recv()
        far_back[dz].wait_recv()
        total = (
            part_y[dz, 0].astype(jnp.float32)
            + near_in[dz].astype(jnp.float32)
            + far_in[dz].astype(jnp.float32)
        )
        if dz:
            col_out[dz] = total.astype(jnp.bfloat16)
            z_back[dz - 1].start()
        else:
            acc[...] = total

    dequant_in(0)
    pass_diag(0)
    pass_on(1)
    dequant_in(1)
    pass_on(2)
    gate_up(0)
    pass_diag(1)
    dequant_down()
    pass_on(3)
    gate_up(1)
    pass_diag(2)
    for cp in rows_sent:
        cp.wait_recv()
    down(0)
    back(0)
    gate_up(2)
    pass_diag(3)
    turn(0)
    down(1)
    back(1)
    gate_up(3)
    turn(1)
    down(2)
    back(2)
    column_sum(0)
    down(3)
    back(3)
    column_sum(1)
    turn(2)
    turn(3)
    column_sum(2)
    column_sum(3)
    for dz in range(1, 4):
        z_back[dz - 1].wait_recv()
        acc[...] += z_in[dz].astype(jnp.float32)
    out_ref[...] = acc[...].astype(jnp.bfloat16)

    for cp in (
        tok_z + rows_sent + parts + tok_diag + diag_back + near_back + far_back + z_back
        + [cp for pair in tok_xy for cp in pair]
    ):
        cp.wait_send()


def fused_local(
    tokens, expert_ids, route_weights, gate_q, up_q, down_q, gate_scale, up_scale, down_scale
):
    rows, half = tokens.shape
    ff = gate_q.shape[2]
    bf16, f32 = jnp.bfloat16, jnp.float32
    vmem = pl.BlockSpec(memory_space=pltpu.VMEM)
    hbm = pl.BlockSpec(memory_space=pl.ANY)
    dma = pltpu.SemaphoreType.DMA
    return pl.pallas_call(
        fused_kernel,
        out_shape=jax.ShapeDtypeStruct((rows, half), bf16),
        in_specs=[vmem] * 6 + [hbm] * 3,
        out_specs=vmem,
        scratch_shapes=[
            pltpu.VMEM((4, 4, rows, half), bf16),
            pltpu.VMEM((2, half, ff), bf16),
            pltpu.VMEM((ff, half), bf16),
            pltpu.VMEM((2, 16, ff), f32),
            pltpu.VMEM((ff // 128, half), f32),
            pltpu.VMEM((2, 2, 4 * rows, ff), f32),
            pltpu.VMEM((4, 2, 4 * rows, ff), bf16),
            pltpu.VMEM((4, 2, 4 * rows, ff), bf16),
            pltpu.VMEM((4 * rows, ff), bf16),
            pltpu.VMEM((4, 4, rows, half), bf16),
            pltpu.VMEM((4, rows, half), bf16),
            pltpu.VMEM((4, rows, half), bf16),
            pltpu.VMEM((4, rows, half), bf16),
            pltpu.VMEM((4, rows, half), bf16),
            pltpu.VMEM((4, rows, half), bf16),
            pltpu.VMEM((rows, half), f32),
            pltpu.VMEM((16, 8, 128), f32),
            pltpu.VMEM((16, 8, 128), f32),
            dma((3,)),
            dma((4, 4)),
            dma((4, 4)),
            dma((4,)),
            dma((4,)),
            dma((16,)),
            dma((16,)),
            dma((3, 4)),
            dma((3, 4)),
            dma((4,)),
            dma((4,)),
        ],
        compiler_params=pltpu.CompilerParams(
            collective_id=0, has_side_effects=True, vmem_limit_bytes=58 * 1024 * 1024
        ),
        cost_estimate=pl.CostEstimate(
            flops=2 * 16 * rows * half * ff * 3,
            bytes_accessed=3 * 2 * half * ff,
            transcendentals=16 * rows * ff,
        ),
    )(
        tokens, expert_ids.T, route_weights.T, gate_scale.swapaxes(1, 2), up_scale.swapaxes(1, 2),
        down_scale, gate_q, up_q, down_q,
    )


def solution(mesh):
    return jax.shard_map(
        fused_local if mesh.shape["expert"] == 16 and mesh.shape["tensor"] == 2 else exchange_local,
        mesh=mesh,
        in_specs=(
            P(("groups", "expert"), "tensor"),
            P(("groups", "expert"), None),
            P(("groups", "expert"), None),
            P("expert", "tensor", None),
            P("expert", "tensor", None),
            P("expert", None, "tensor"),
            P("expert", "tensor", None),
            P("expert", "tensor", None),
            P("expert", None, "tensor"),
        ),
        out_specs=P(("groups", "expert"), "tensor"),
        check_vma=False,
    )
```

```python
import jax
import jax.numpy as jnp
from jax import lax
from jax.experimental import pallas as pl
from jax.experimental.pallas import tpu as pltpu
from jax.sharding import PartitionSpec as P

FF = 1024


def dequant(quant, scales):
    height, breadth = quant.shape
    blocks = (
        quant.reshape(height // 128, 128, breadth // 128, 128).astype(jnp.float32)
        * scales[:, None, :, None]
    )
    return blocks.reshape(height, breadth).astype(jnp.bfloat16)


def exchange_local(
    tokens, expert_ids, route_weights, gate_q, up_q, down_q, gate_scale, up_scale, down_scale
):
    holders = lax.axis_size("expert")
    tok_rows, half_width = tokens.shape
    pick_count = expert_ids.shape[1]
    slices = FF // gate_q.shape[2]
    experts = holders // slices
    capacity = max(
        2, min(tok_rows, tok_rows * pick_count // experts + tok_rows * pick_count // (8 * experts))
    )
    slot_range = experts * capacity
    flat_ids = expert_ids.reshape(-1)
    onehot = (flat_ids[:, None] == jnp.arange(experts)[None, :]).astype(jnp.int32)
    before = jnp.cumsum(onehot, axis=0) - onehot
    position = jnp.sum(before * onehot, axis=1)
    slot_ids = flat_ids * capacity + position
    placing = (slot_ids[:, None] == jnp.arange(slot_range)[None, :]).astype(jnp.int32)
    pair_owner = jnp.arange(tok_rows * pick_count, dtype=jnp.int32) // pick_count
    token_of_slot = jnp.sum(placing * pair_owner[:, None], axis=0)
    occupied = jnp.sum(placing, axis=0) > 0
    filled = jnp.where(occupied[:, None], tokens[token_of_slot], jnp.zeros((), jnp.bfloat16))
    w_gate = dequant(gate_q[0], gate_scale[0])
    w_up = dequant(up_q[0], up_scale[0])
    w_down = dequant(down_q[0], down_scale[0])
    ff_width = w_gate.shape[1]
    outgoing = jnp.repeat(filled.reshape(experts, capacity, half_width), slices, axis=0)
    received = lax.all_to_all(outgoing, "expert", split_axis=0, concat_axis=0, tiled=True)
    sources, slots_here, _ = received.shape
    row_block = received.reshape(sources * slots_here, half_width)
    partial_value = jnp.concatenate(
        [
            jnp.dot(row_block, w_gate, preferred_element_type=jnp.float32),
            jnp.dot(row_block, w_up, preferred_element_type=jnp.float32),
        ],
        axis=1,
    )
    summed = lax.psum(partial_value, "tensor")
    hidden = (jax.nn.silu(summed[:, :ff_width]) * summed[:, ff_width:]).astype(jnp.bfloat16)
    term = jnp.dot(hidden, w_down, preferred_element_type=jnp.float32)
    result = term.astype(jnp.bfloat16).astype(jnp.float32)
    result = result.astype(jnp.bfloat16)
    returned = lax.all_to_all(
        result.reshape(sources, slots_here, half_width),
        "expert",
        split_axis=0,
        concat_axis=0,
        tiled=True,
    )
    combined = jnp.sum(
        returned.reshape(experts, slices, capacity, half_width).astype(jnp.float32), axis=1
    )
    rounded = lax.optimization_barrier(combined.astype(jnp.bfloat16)).astype(jnp.float32)
    flat_back = rounded.reshape(slot_range, half_width)
    picked = flat_back[slot_ids].reshape(tok_rows, pick_count, half_width)
    routed = jnp.zeros((tok_rows, half_width), jnp.float32)
    for column in range(pick_count):
        routed = routed + route_weights[:, column : column + 1] * picked[:, column]
    return routed.astype(jnp.bfloat16)


MESH = pl.DeviceIdType.MESH
ROWS = 64


def peer(e, d):
    out = e
    for bit in (1, 2, 4, 8):
        if d & bit:
            out = out + bit - 2 * bit * ((e // bit) % 2)
    return out


def fused_kernel(
    tok_ref, ids_ref, rw_ref, gs_ref, us_ref, ds_ref, gate_hbm, up_hbm, down_hbm, out_ref,
    tok, w_in, w_down, scale_in, scale_down, part_own, part_out, part_in, hid, part_y,
    diag_in, near_in, far_in, col_out, z_in, acc, wrow_out, wrow_in,
    load_sem, tok_send, tok_recv, part_send, part_recv, row_send, row_recv,
    y_send, y_recv, z_send, z_recv,
):
    e = lax.axis_index("expert")
    c = lax.axis_index("tensor")
    half = tok_ref.shape[1]
    ff = w_down.shape[0]
    loads = [
        pltpu.make_async_copy(gate_hbm.at[0], w_in.at[0], load_sem.at[0]),
        pltpu.make_async_copy(up_hbm.at[0], w_in.at[1], load_sem.at[1]),
        pltpu.make_async_copy(down_hbm.at[0], w_down, load_sem.at[2]),
    ]
    for load in loads:
        load.start()

    barrier = pltpu.get_barrier_semaphore()
    for d in range(1, 16):
        pl.semaphore_signal(barrier, inc=1, device_id={"expert": peer(e, d)}, device_id_type=MESH)
    pl.semaphore_signal(barrier, inc=1, device_id={"tensor": 1 - c}, device_id_type=MESH)

    eye = lax.broadcasted_iota(jnp.int32, (ROWS, ROWS), 0) == lax.broadcasted_iota(
        jnp.int32, (ROWS, ROWS), 1
    )
    ids = ids_ref[...]
    rw = rw_ref[...]
    for d in range(16):
        row = jnp.sum(jnp.where(ids == peer(e, d), rw, 0.0), axis=0, keepdims=True)
        wrow_out[d, :, 0:ROWS] = jnp.broadcast_to(row, (8, ROWS))
    tok[0, 0] = tok_ref[...]
    pl.semaphore_wait(barrier, 16)

    def send(src, dst, s_sem, r_sem, **where):
        return pltpu.make_async_remote_copy(
            src_ref=src, dst_ref=dst, send_sem=s_sem, recv_sem=r_sem,
            device_id=where, device_id_type=MESH,
        )

    tok_z = [
        send(tok_ref, tok.at[dz, 0], tok_send.at[dz, 0], tok_recv.at[dz, 0], expert=peer(e, 4 * dz))
        for dz in range(1, 4)
    ]
    tok_xy = [
        [
            send(
                tok.at[dz, 0] if dz else tok_ref, tok.at[dz, k], tok_send.at[dz, k],
                tok_recv.at[dz, k], expert=peer(e, k),
            )
            for k in (1, 2)
        ]
        for dz in range(4)
    ]
    near = 1 + c
    far = 2 - c
    near_dev = e + (1 - c) * (1 - 2 * (e % 2)) + c * (2 - 4 * ((e // 2) % 2))
    far_dev = e + c * (1 - 2 * (e % 2)) + (1 - c) * (2 - 4 * ((e // 2) % 2))
    tok_diag = [
        send(tok.at[dz, near], tok.at[dz, 3], tok_send.at[dz, 3], tok_recv.at[dz, 3], expert=far_dev)
        for dz in range(4)
    ]

    def wait_tok(k, dz):
        send(tok.at[dz, k], tok.at[dz, k], tok_send.at[0, 0], tok_recv.at[dz, k], expert=near_dev).wait_recv()

    for cp in tok_xy[0]:
        cp.start()
    tok_z[0].start()
    tok_z[1].start()
    rows_sent = [
        send(wrow_out.at[d], wrow_in.at[d], row_send.at[d], row_recv.at[d], expert=peer(e, d))
        for d in range(1, 16)
    ]

    wrow_in[0] = wrow_out[0]
    square = (half // 128, half // 128)
    diagonal = lax.broadcasted_iota(jnp.int32, square, 0) == lax.broadcasted_iota(jnp.int32, square, 1)
    for g, ref in ((0, gs_ref), (1, us_ref)):
        blocks = ref[0]
        for j in range(ff // 128):
            row = blocks[j : j + 1, :]
            column = jnp.sum(jnp.where(diagonal, row, 0.0), axis=1, keepdims=True)
            scale_in[g, 0 : half // 128, j * 128 : (j + 1) * 128] = jnp.broadcast_to(
                column, (half // 128, 128)
            )
    blocks = ds_ref[0]
    for j in range(half // 128):
        scale_down[:, j * 128 : (j + 1) * 128] = jnp.broadcast_to(blocks[:, j : j + 1], (ff // 128, 128))

    def dequant_in(g):
        loads[g].wait()

        @pl.loop(0, half // 128)
        def _(i):
            at = pl.ds(pl.multiple_of(i * 128, 128), 128)
            w_in[g, at, :] = (w_in[g, at, :].astype(jnp.float32) * scale_in[g, pl.ds(i, 1), :]).astype(jnp.bfloat16)

    def dequant_down():
        loads[2].wait()

        @pl.loop(0, ff // 128)
        def _(i):
            at = pl.ds(pl.multiple_of(i * 128, 128), 128)
            w_down[at, :] = (w_down[at, :].astype(jnp.float32) * scale_down[pl.ds(i, 1), :]).astype(jnp.bfloat16)

    def pass_on(dz):
        tok_z[dz - 1].wait_recv()
        if dz == 2:
            tok_z[2].start()
        for cp in tok_xy[dz]:
            cp.start()

    def pass_diag(dz):
        wait_tok(near, dz)
        tok_diag[dz].start()

    parts = [
        send(part_out.at[k], part_in.at[k], part_send.at[k], part_recv.at[k], tensor=1 - c)
        for k in range(4)
    ]

    def gate_up(k):
        wait_tok(far, k)
        tok_diag[k].wait_recv()
        x = tok[k].reshape(4 * ROWS, half)

        @pl.loop(0, 2 * ff // 256)
        def _(t):
            g = t // (ff // 256)
            at = pl.ds(pl.multiple_of((t % (ff // 256)) * 256, 256), 256)
            p = jnp.dot(x, w_in[g, :, at], preferred_element_type=jnp.float32)
            part_own[k % 2, g, :, at] = p
            part_out[k, g, :, at] = p.astype(jnp.bfloat16)

        parts[k].start()

    def down(k):
        parts[k].wait_recv()

        @pl.loop(0, ff // 256)
        def _(t):
            at = pl.ds(pl.multiple_of(t * 256, 256), 256)
            gate = part_own[k % 2, 0, :, at] + part_in[k, 0, :, at].astype(jnp.float32)
            up = part_own[k % 2, 1, :, at] + part_in[k, 1, :, at].astype(jnp.float32)
            hid[:, at] = (gate / (1.0 + jnp.exp(-gate)) * up).astype(jnp.bfloat16)

        columns = []
        for d in range(4):
            row = wrow_in[4 * k + d, 0:1, 0:ROWS]
            columns.append(jnp.sum(jnp.where(eye, row, 0.0), axis=1, keepdims=True))
        column = jnp.concatenate(columns, axis=0)
        h = hid[...]

        @pl.loop(0, half // 256)
        def _(t):
            at = pl.ds(pl.multiple_of(t * 256, 256), 256)
            y = jnp.dot(h, w_down[:, at], preferred_element_type=jnp.float32) * column
            part_y[k, :, :, at] = y.reshape(4, ROWS, 256).astype(jnp.bfloat16)

    diag_back = [
        send(part_y.at[dz, 3], diag_in.at[dz], y_send.at[0, dz], y_recv.at[0, dz], expert=near_dev)
        for dz in range(4)
    ]
    near_back = [
        send(part_y.at[dz, near], near_in.at[dz], y_send.at[1, dz], y_recv.at[1, dz], expert=near_dev)
        for dz in range(4)
    ]
    far_back = [
        send(part_y.at[dz, far], far_in.at[dz], y_send.at[2, dz], y_recv.at[2, dz], expert=far_dev)
        for dz in range(4)
    ]
    z_back = [
        send(col_out.at[dz], z_in.at[dz], z_send.at[dz], z_recv.at[dz], expert=peer(e, 4 * dz))
        for dz in range(1, 4)
    ]

    def back(dz):
        near_back[dz].start()
        diag_back[dz].start()

    def turn(dz):
        diag_back[dz].wait_recv()
        part_y[dz, far] = (
            part_y[dz, far].astype(jnp.float32) + diag_in[dz].astype(jnp.float32)
        ).astype(jnp.bfloat16)
        far_back[dz].start()

    def column_sum(dz):
        near_back[dz].wait_recv()
        far_back[dz].wait_recv()
        total = (
            part_y[dz, 0].astype(jnp.float32)
            + near_in[dz].astype(jnp.float32)
            + far_in[dz].astype(jnp.float32)
        )
        if dz:
            col_out[dz] = total.astype(jnp.bfloat16)
            z_back[dz - 1].start()
        else:
            acc[...] = total

    pass_diag(0)
    pass_on(1)
    for cp in rows_sent:
        cp.start()
    dequant_in(0)
    dequant_in(1)
    pass_on(2)
    gate_up(0)
    pass_diag(1)
    dequant_down()
    for cp in rows_sent:
        cp.wait_recv()
    down(0)
    back(0)
    pass_diag(2)
    gate_up(1)
    turn(0)
    down(1)
    gate_up(2)
    pass_on(3)
    down(2)
    back(2)
    pass_diag(3)
    turn(2)
    column_sum(0)
    gate_up(3)
    column_sum(2)
    down(3)
    back(3)
    back(1)
    turn(3)
    turn(1)
    column_sum(3)
    column_sum(1)
    for dz in range(1, 4):
        z_back[dz - 1].wait_recv()
        acc[...] += z_in[dz].astype(jnp.float32)
    out_ref[...] = acc[...].astype(jnp.bfloat16)

    for cp in (
        tok_z + rows_sent + parts + tok_diag + diag_back + near_back + far_back + z_back
        + [cp for pair in tok_xy for cp in pair]
    ):
        cp.wait_send()


def fused_local(
    tokens, expert_ids, route_weights, gate_q, up_q, down_q, gate_scale, up_scale, down_scale
):
    rows, half = tokens.shape
    ff = gate_q.shape[2]
    bf16, f32 = jnp.bfloat16, jnp.float32
    vmem = pl.BlockSpec(memory_space=pltpu.VMEM)
    hbm = pl.BlockSpec(memory_space=pl.ANY)
    dma = pltpu.SemaphoreType.DMA
    return pl.pallas_call(
        fused_kernel,
        out_shape=jax.ShapeDtypeStruct((rows, half), bf16),
        in_specs=[vmem] * 6 + [hbm] * 3,
        out_specs=vmem,
        scratch_shapes=[
            pltpu.VMEM((4, 4, rows, half), bf16),
            pltpu.VMEM((2, half, ff), bf16),
            pltpu.VMEM((ff, half), bf16),
            pltpu.VMEM((2, 16, ff), f32),
            pltpu.VMEM((ff // 128, half), f32),
            pltpu.VMEM((2, 2, 4 * rows, ff), f32),
            pltpu.VMEM((4, 2, 4 * rows, ff), bf16),
            pltpu.VMEM((4, 2, 4 * rows, ff), bf16),
            pltpu.VMEM((4 * rows, ff), bf16),
            pltpu.VMEM((4, 4, rows, half), bf16),
            pltpu.VMEM((4, rows, half), bf16),
            pltpu.VMEM((4, rows, half), bf16),
            pltpu.VMEM((4, rows, half), bf16),
            pltpu.VMEM((4, rows, half), bf16),
            pltpu.VMEM((4, rows, half), bf16),
            pltpu.VMEM((rows, half), f32),
            pltpu.VMEM((16, 8, 128), f32),
            pltpu.VMEM((16, 8, 128), f32),
            dma((3,)),
            dma((4, 4)),
            dma((4, 4)),
            dma((4,)),
            dma((4,)),
            dma((16,)),
            dma((16,)),
            dma((3, 4)),
            dma((3, 4)),
            dma((4,)),
            dma((4,)),
        ],
        compiler_params=pltpu.CompilerParams(
            collective_id=0, has_side_effects=True, vmem_limit_bytes=58 * 1024 * 1024
        ),
        cost_estimate=pl.CostEstimate(
            flops=2 * 16 * rows * half * ff * 3,
            bytes_accessed=3 * 2 * half * ff,
            transcendentals=16 * rows * ff,
        ),
    )(
        tokens, expert_ids.T, route_weights.T, gate_scale.swapaxes(1, 2), up_scale.swapaxes(1, 2),
        down_scale, gate_q, up_q, down_q,
    )


def solution(mesh):
    return jax.shard_map(
        fused_local if mesh.shape["expert"] == 16 and mesh.shape["tensor"] == 2 else exchange_local,
        mesh=mesh,
        in_specs=(
            P(("groups", "expert"), "tensor"),
            P(("groups", "expert"), None),
            P(("groups", "expert"), None),
            P("expert", "tensor", None),
            P("expert", "tensor", None),
            P("expert", None, "tensor"),
            P("expert", "tensor", None),
            P("expert", "tensor", None),
            P("expert", None, "tensor"),
        ),
        out_specs=P(("groups", "expert"), "tensor"),
        check_vma=False,
    )
```

```python
import jax
import jax.numpy as jnp
from jax import lax
from jax.experimental import pallas as pl
from jax.experimental.pallas import tpu as pltpu
from jax.sharding import PartitionSpec as P

FF = 1024


def dequant(quant, scales):
    height, breadth = quant.shape
    blocks = (
        quant.reshape(height // 128, 128, breadth // 128, 128).astype(jnp.float32)
        * scales[:, None, :, None]
    )
    return blocks.reshape(height, breadth).astype(jnp.bfloat16)


def exchange_local(
    tokens, expert_ids, route_weights, gate_q, up_q, down_q, gate_scale, up_scale, down_scale
):
    holders = lax.axis_size("expert")
    tok_rows, half_width = tokens.shape
    pick_count = expert_ids.shape[1]
    slices = FF // gate_q.shape[2]
    experts = holders // slices
    capacity = max(
        2, min(tok_rows, tok_rows * pick_count // experts + tok_rows * pick_count // (8 * experts))
    )
    slot_range = experts * capacity
    flat_ids = expert_ids.reshape(-1)
    onehot = (flat_ids[:, None] == jnp.arange(experts)[None, :]).astype(jnp.int32)
    before = jnp.cumsum(onehot, axis=0) - onehot
    position = jnp.sum(before * onehot, axis=1)
    slot_ids = flat_ids * capacity + position
    placing = (slot_ids[:, None] == jnp.arange(slot_range)[None, :]).astype(jnp.int32)
    pair_owner = jnp.arange(tok_rows * pick_count, dtype=jnp.int32) // pick_count
    token_of_slot = jnp.sum(placing * pair_owner[:, None], axis=0)
    occupied = jnp.sum(placing, axis=0) > 0
    filled = jnp.where(occupied[:, None], tokens[token_of_slot], jnp.zeros((), jnp.bfloat16))
    w_gate = dequant(gate_q[0], gate_scale[0])
    w_up = dequant(up_q[0], up_scale[0])
    w_down = dequant(down_q[0], down_scale[0])
    ff_width = w_gate.shape[1]
    outgoing = jnp.repeat(filled.reshape(experts, capacity, half_width), slices, axis=0)
    received = lax.all_to_all(outgoing, "expert", split_axis=0, concat_axis=0, tiled=True)
    sources, slots_here, _ = received.shape
    row_block = received.reshape(sources * slots_here, half_width)
    partial_value = jnp.concatenate(
        [
            jnp.dot(row_block, w_gate, preferred_element_type=jnp.float32),
            jnp.dot(row_block, w_up, preferred_element_type=jnp.float32),
        ],
        axis=1,
    )
    summed = lax.psum(partial_value, "tensor")
    hidden = (jax.nn.silu(summed[:, :ff_width]) * summed[:, ff_width:]).astype(jnp.bfloat16)
    term = jnp.dot(hidden, w_down, preferred_element_type=jnp.float32)
    result = term.astype(jnp.bfloat16).astype(jnp.float32)
    result = result.astype(jnp.bfloat16)
    returned = lax.all_to_all(
        result.reshape(sources, slots_here, half_width),
        "expert",
        split_axis=0,
        concat_axis=0,
        tiled=True,
    )
    combined = jnp.sum(
        returned.reshape(experts, slices, capacity, half_width).astype(jnp.float32), axis=1
    )
    rounded = lax.optimization_barrier(combined.astype(jnp.bfloat16)).astype(jnp.float32)
    flat_back = rounded.reshape(slot_range, half_width)
    picked = flat_back[slot_ids].reshape(tok_rows, pick_count, half_width)
    routed = jnp.zeros((tok_rows, half_width), jnp.float32)
    for column in range(pick_count):
        routed = routed + route_weights[:, column : column + 1] * picked[:, column]
    return routed.astype(jnp.bfloat16)


MESH = pl.DeviceIdType.MESH
ROWS = 64


def peer(e, d):
    out = e
    for bit in (1, 2, 4, 8):
        if d & bit:
            out = out + bit - 2 * bit * ((e // bit) % 2)
    return out


def fused_kernel(
    tok_ref, ids_ref, rw_ref, gs_ref, us_ref, ds_ref, gate_hbm, up_hbm, down_hbm, out_ref,
    tok, w_in, w_down, scale_in, scale_down, part_own, part_out, part_in, hid, part_y,
    diag_in, near_in, far_in, col_out, z_in, acc, wrow_out, wrow_in,
    load_sem, tok_send, tok_recv, part_send, part_recv, row_send, row_recv,
    y_send, y_recv, z_send, z_recv,
):
    e = lax.axis_index("expert")
    c = lax.axis_index("tensor")
    half = tok_ref.shape[1]
    ff = w_down.shape[0]
    loads = [
        pltpu.make_async_copy(gate_hbm.at[0], w_in.at[0], load_sem.at[0]),
        pltpu.make_async_copy(up_hbm.at[0], w_in.at[1], load_sem.at[1]),
        pltpu.make_async_copy(down_hbm.at[0], w_down, load_sem.at[2]),
    ]
    for load in loads:
        load.start()

    barrier = pltpu.get_barrier_semaphore()
    for d in range(1, 16):
        pl.semaphore_signal(barrier, inc=1, device_id={"expert": peer(e, d)}, device_id_type=MESH)
    pl.semaphore_signal(barrier, inc=1, device_id={"tensor": 1 - c}, device_id_type=MESH)

    eye = lax.broadcasted_iota(jnp.int32, (ROWS, ROWS), 0) == lax.broadcasted_iota(
        jnp.int32, (ROWS, ROWS), 1
    )
    ids = ids_ref[...]
    rw = rw_ref[...]
    for d in range(16):
        row = jnp.sum(jnp.where(ids == peer(e, d), rw, 0.0), axis=0, keepdims=True)
        wrow_out[d, :, 0:ROWS] = jnp.broadcast_to(row, (8, ROWS))
    tok[0, 0] = tok_ref[...]
    pl.semaphore_wait(barrier, 16)

    def send(src, dst, s_sem, r_sem, **where):
        return pltpu.make_async_remote_copy(
            src_ref=src, dst_ref=dst, send_sem=s_sem, recv_sem=r_sem,
            device_id=where, device_id_type=MESH,
        )

    tok_z = [
        send(tok_ref, tok.at[dz, 0], tok_send.at[dz, 0], tok_recv.at[dz, 0], expert=peer(e, 4 * dz))
        for dz in range(1, 4)
    ]
    tok_xy = [
        [
            send(
                tok.at[dz, 0] if dz else tok_ref, tok.at[dz, k], tok_send.at[dz, k],
                tok_recv.at[dz, k], expert=peer(e, k),
            )
            for k in (1, 2)
        ]
        for dz in range(4)
    ]
    near = 1 + c
    far = 2 - c
    near_dev = e + (1 - c) * (1 - 2 * (e % 2)) + c * (2 - 4 * ((e // 2) % 2))
    far_dev = e + c * (1 - 2 * (e % 2)) + (1 - c) * (2 - 4 * ((e // 2) % 2))
    tok_diag = [
        send(tok.at[dz, near], tok.at[dz, 3], tok_send.at[dz, 3], tok_recv.at[dz, 3], expert=far_dev)
        for dz in range(4)
    ]

    def wait_tok(k, dz):
        send(tok.at[dz, k], tok.at[dz, k], tok_send.at[0, 0], tok_recv.at[dz, k], expert=near_dev).wait_recv()

    for cp in tok_xy[0]:
        cp.start()
    for cp in tok_z:
        cp.start()
    rows_sent = [
        send(wrow_out.at[d], wrow_in.at[d], row_send.at[d], row_recv.at[d], expert=peer(e, d))
        for d in range(1, 16)
    ]

    wrow_in[0] = wrow_out[0]
    square = (half // 128, half // 128)
    diagonal = lax.broadcasted_iota(jnp.int32, square, 0) == lax.broadcasted_iota(jnp.int32, square, 1)
    for g, ref in ((0, gs_ref), (1, us_ref)):
        blocks = ref[0]
        for j in range(ff // 128):
            row = blocks[j : j + 1, :]
            column = jnp.sum(jnp.where(diagonal, row, 0.0), axis=1, keepdims=True)
            scale_in[g, 0 : half // 128, j * 128 : (j + 1) * 128] = jnp.broadcast_to(
                column, (half // 128, 128)
            )
    blocks = ds_ref[0]
    for j in range(half // 128):
        scale_down[:, j * 128 : (j + 1) * 128] = jnp.broadcast_to(blocks[:, j : j + 1], (ff // 128, 128))

    def dequant_in(g):
        loads[g].wait()

        @pl.loop(0, half // 128)
        def _(i):
            at = pl.ds(pl.multiple_of(i * 128, 128), 128)
            w_in[g, at, :] = (w_in[g, at, :].astype(jnp.float32) * scale_in[g, pl.ds(i, 1), :]).astype(jnp.bfloat16)

    def dequant_down():
        loads[2].wait()

        @pl.loop(0, ff // 128)
        def _(i):
            at = pl.ds(pl.multiple_of(i * 128, 128), 128)
            w_down[at, :] = (w_down[at, :].astype(jnp.float32) * scale_down[pl.ds(i, 1), :]).astype(jnp.bfloat16)

    def pass_on(dz):
        tok_z[dz - 1].wait_recv()
        for cp in tok_xy[dz]:
            cp.start()

    def pass_diag(dz):
        wait_tok(near, dz)
        tok_diag[dz].start()

    parts = [
        send(part_out.at[k], part_in.at[k], part_send.at[k], part_recv.at[k], tensor=1 - c)
        for k in range(4)
    ]

    def gate_up(k):
        wait_tok(far, k)
        tok_diag[k].wait_recv()
        x = tok[k].reshape(4 * ROWS, half)

        @pl.loop(0, 2 * ff // 256)
        def _(t):
            g = t // (ff // 256)
            at = pl.ds(pl.multiple_of((t % (ff // 256)) * 256, 256), 256)
            p = jnp.dot(x, w_in[g, :, at], preferred_element_type=jnp.float32)
            part_own[k % 2, g, :, at] = p
            part_out[k, g, :, at] = p.astype(jnp.bfloat16)

        parts[k].start()

    def down(k):
        parts[k].wait_recv()

        @pl.loop(0, ff // 256)
        def _(t):
            at = pl.ds(pl.multiple_of(t * 256, 256), 256)
            gate = part_own[k % 2, 0, :, at] + part_in[k, 0, :, at].astype(jnp.float32)
            up = part_own[k % 2, 1, :, at] + part_in[k, 1, :, at].astype(jnp.float32)
            hid[:, at] = (gate / (1.0 + jnp.exp(-gate)) * up).astype(jnp.bfloat16)

        columns = []
        for d in range(4):
            row = wrow_in[4 * k + d, 0:1, 0:ROWS]
            columns.append(jnp.sum(jnp.where(eye, row, 0.0), axis=1, keepdims=True))
        column = jnp.concatenate(columns, axis=0)
        h = hid[...]

        @pl.loop(0, half // 256)
        def _(t):
            at = pl.ds(pl.multiple_of(t * 256, 256), 256)
            y = jnp.dot(h, w_down[:, at], preferred_element_type=jnp.float32) * column
            part_y[k, :, :, at] = y.reshape(4, ROWS, 256).astype(jnp.bfloat16)

    diag_back = [
        send(part_y.at[dz, 3], diag_in.at[dz], y_send.at[0, dz], y_recv.at[0, dz], expert=near_dev)
        for dz in range(4)
    ]
    near_back = [
        send(part_y.at[dz, near], near_in.at[dz], y_send.at[1, dz], y_recv.at[1, dz], expert=near_dev)
        for dz in range(4)
    ]
    far_back = [
        send(part_y.at[dz, far], far_in.at[dz], y_send.at[2, dz], y_recv.at[2, dz], expert=far_dev)
        for dz in range(4)
    ]
    z_back = [
        send(col_out.at[dz], z_in.at[dz], z_send.at[dz], z_recv.at[dz], expert=peer(e, 4 * dz))
        for dz in range(1, 4)
    ]

    def back(dz):
        near_back[dz].start()
        diag_back[dz].start()

    def turn(dz):
        diag_back[dz].wait_recv()
        part_y[dz, far] = (
            part_y[dz, far].astype(jnp.float32) + diag_in[dz].astype(jnp.float32)
        ).astype(jnp.bfloat16)
        far_back[dz].start()

    def column_sum(dz):
        near_back[dz].wait_recv()
        far_back[dz].wait_recv()
        total = (
            part_y[dz, 0].astype(jnp.float32)
            + near_in[dz].astype(jnp.float32)
            + far_in[dz].astype(jnp.float32)
        )
        if dz:
            col_out[dz] = total.astype(jnp.bfloat16)
            z_back[dz - 1].start()
        else:
            acc[...] = total

    dequant_in(0)
    pass_diag(0)
    pass_on(1)
    for cp in rows_sent:
        cp.start()
    dequant_in(1)
    pass_on(2)
    gate_up(0)
    pass_diag(1)
    dequant_down()
    pass_on(3)
    gate_up(1)
    pass_diag(2)
    for cp in rows_sent:
        cp.wait_recv()
    down(0)
    back(0)
    gate_up(2)
    pass_diag(3)
    turn(0)
    down(1)
    back(1)
    gate_up(3)
    turn(1)
    down(2)
    back(2)
    column_sum(0)
    down(3)
    back(3)
    column_sum(1)
    turn(2)
    column_sum(2)
    turn(3)
    column_sum(3)
    for dz in range(1, 4):
        z_back[dz - 1].wait_recv()
        acc[...] += z_in[dz].astype(jnp.float32)
    out_ref[...] = acc[...].astype(jnp.bfloat16)

    for cp in (
        tok_z + rows_sent + parts + tok_diag + diag_back + near_back + far_back + z_back
        + [cp for pair in tok_xy for cp in pair]
    ):
        cp.wait_send()


def fused_local(
    tokens, expert_ids, route_weights, gate_q, up_q, down_q, gate_scale, up_scale, down_scale
):
    rows, half = tokens.shape
    ff = gate_q.shape[2]
    bf16, f32 = jnp.bfloat16, jnp.float32
    vmem = pl.BlockSpec(memory_space=pltpu.VMEM)
    hbm = pl.BlockSpec(memory_space=pl.ANY)
    dma = pltpu.SemaphoreType.DMA
    return pl.pallas_call(
        fused_kernel,
        out_shape=jax.ShapeDtypeStruct((rows, half), bf16),
        in_specs=[vmem] * 6 + [hbm] * 3,
        out_specs=vmem,
        scratch_shapes=[
            pltpu.VMEM((4, 4, rows, half), bf16),
            pltpu.VMEM((2, half, ff), bf16),
            pltpu.VMEM((ff, half), bf16),
            pltpu.VMEM((2, 16, ff), f32),
            pltpu.VMEM((ff // 128, half), f32),
            pltpu.VMEM((2, 2, 4 * rows, ff), f32),
            pltpu.VMEM((4, 2, 4 * rows, ff), bf16),
            pltpu.VMEM((4, 2, 4 * rows, ff), bf16),
            pltpu.VMEM((4 * rows, ff), bf16),
            pltpu.VMEM((4, 4, rows, half), bf16),
            pltpu.VMEM((4, rows, half), bf16),
            pltpu.VMEM((4, rows, half), bf16),
            pltpu.VMEM((4, rows, half), bf16),
            pltpu.VMEM((4, rows, half), bf16),
            pltpu.VMEM((4, rows, half), bf16),
            pltpu.VMEM((rows, half), f32),
            pltpu.VMEM((16, 8, 128), f32),
            pltpu.VMEM((16, 8, 128), f32),
            dma((3,)),
            dma((4, 4)),
            dma((4, 4)),
            dma((4,)),
            dma((4,)),
            dma((16,)),
            dma((16,)),
            dma((3, 4)),
            dma((3, 4)),
            dma((4,)),
            dma((4,)),
        ],
        compiler_params=pltpu.CompilerParams(
            collective_id=0, has_side_effects=True, vmem_limit_bytes=58 * 1024 * 1024
        ),
        cost_estimate=pl.CostEstimate(
            flops=2 * 16 * rows * half * ff * 3,
            bytes_accessed=3 * 2 * half * ff,
            transcendentals=16 * rows * ff,
        ),
    )(
        tokens, expert_ids.T, route_weights.T, gate_scale.swapaxes(1, 2), up_scale.swapaxes(1, 2),
        down_scale, gate_q, up_q, down_q,
    )


def solution(mesh):
    return jax.shard_map(
        fused_local if mesh.shape["expert"] == 16 and mesh.shape["tensor"] == 2 else exchange_local,
        mesh=mesh,
        in_specs=(
            P(("groups", "expert"), "tensor"),
            P(("groups", "expert"), None),
            P(("groups", "expert"), None),
            P("expert", "tensor", None),
            P("expert", "tensor", None),
            P("expert", None, "tensor"),
            P("expert", "tensor", None),
            P("expert", "tensor", None),
            P("expert", None, "tensor"),
        ),
        out_specs=P(("groups", "expert"), "tensor"),
        check_vma=False,
    )
```

```python
import jax
import jax.numpy as jnp
from jax import lax
from jax.experimental import pallas as pl
from jax.experimental.pallas import tpu as pltpu
from jax.sharding import PartitionSpec as P

FF = 1024


def dequant(quant, scales):
    height, breadth = quant.shape
    blocks = (
        quant.reshape(height // 128, 128, breadth // 128, 128).astype(jnp.float32)
        * scales[:, None, :, None]
    )
    return blocks.reshape(height, breadth).astype(jnp.bfloat16)


def exchange_local(
    tokens, expert_ids, route_weights, gate_q, up_q, down_q, gate_scale, up_scale, down_scale
):
    holders = lax.axis_size("expert")
    tok_rows, half_width = tokens.shape
    pick_count = expert_ids.shape[1]
    slices = FF // gate_q.shape[2]
    experts = holders // slices
    capacity = max(
        2, min(tok_rows, tok_rows * pick_count // experts + tok_rows * pick_count // (8 * experts))
    )
    slot_range = experts * capacity
    flat_ids = expert_ids.reshape(-1)
    onehot = (flat_ids[:, None] == jnp.arange(experts)[None, :]).astype(jnp.int32)
    before = jnp.cumsum(onehot, axis=0) - onehot
    position = jnp.sum(before * onehot, axis=1)
    slot_ids = flat_ids * capacity + position
    placing = (slot_ids[:, None] == jnp.arange(slot_range)[None, :]).astype(jnp.int32)
    pair_owner = jnp.arange(tok_rows * pick_count, dtype=jnp.int32) // pick_count
    token_of_slot = jnp.sum(placing * pair_owner[:, None], axis=0)
    occupied = jnp.sum(placing, axis=0) > 0
    filled = jnp.where(occupied[:, None], tokens[token_of_slot], jnp.zeros((), jnp.bfloat16))
    w_gate = dequant(gate_q[0], gate_scale[0])
    w_up = dequant(up_q[0], up_scale[0])
    w_down = dequant(down_q[0], down_scale[0])
    ff_width = w_gate.shape[1]
    outgoing = jnp.repeat(filled.reshape(experts, capacity, half_width), slices, axis=0)
    received = lax.all_to_all(outgoing, "expert", split_axis=0, concat_axis=0, tiled=True)
    sources, slots_here, _ = received.shape
    row_block = received.reshape(sources * slots_here, half_width)
    partial_value = jnp.concatenate(
        [
            jnp.dot(row_block, w_gate, preferred_element_type=jnp.float32),
            jnp.dot(row_block, w_up, preferred_element_type=jnp.float32),
        ],
        axis=1,
    )
    summed = lax.psum(partial_value, "tensor")
    hidden = (jax.nn.silu(summed[:, :ff_width]) * summed[:, ff_width:]).astype(jnp.bfloat16)
    term = jnp.dot(hidden, w_down, preferred_element_type=jnp.float32)
    result = term.astype(jnp.bfloat16).astype(jnp.float32)
    result = result.astype(jnp.bfloat16)
    returned = lax.all_to_all(
        result.reshape(sources, slots_here, half_width),
        "expert",
        split_axis=0,
        concat_axis=0,
        tiled=True,
    )
    combined = jnp.sum(
        returned.reshape(experts, slices, capacity, half_width).astype(jnp.float32), axis=1
    )
    rounded = lax.optimization_barrier(combined.astype(jnp.bfloat16)).astype(jnp.float32)
    flat_back = rounded.reshape(slot_range, half_width)
    picked = flat_back[slot_ids].reshape(tok_rows, pick_count, half_width)
    routed = jnp.zeros((tok_rows, half_width), jnp.float32)
    for column in range(pick_count):
        routed = routed + route_weights[:, column : column + 1] * picked[:, column]
    return routed.astype(jnp.bfloat16)


MESH = pl.DeviceIdType.MESH
ROWS = 64


def peer(e, d):
    out = e
    for bit in (1, 2, 4, 8):
        if d & bit:
            out = out + bit - 2 * bit * ((e // bit) % 2)
    return out


def fused_kernel(
    tok_ref, ids_ref, rw_ref, gs_ref, us_ref, ds_ref, gate_hbm, up_hbm, down_hbm, out_ref,
    tok, w_in, w_down, scale_in, scale_down, part_own, part_out, part_in, hid, part_y,
    diag_in, near_in, far_in, col_out, z_in, acc, wrow_out, wrow_in,
    load_sem, tok_send, tok_recv, part_send, part_recv, row_send, row_recv,
    y_send, y_recv, z_send, z_recv,
):
    e = lax.axis_index("expert")
    c = lax.axis_index("tensor")
    half = tok_ref.shape[1]
    ff = w_down.shape[0]
    loads = [
        pltpu.make_async_copy(gate_hbm.at[0], w_in.at[0], load_sem.at[0]),
        pltpu.make_async_copy(up_hbm.at[0], w_in.at[1], load_sem.at[1]),
        pltpu.make_async_copy(down_hbm.at[0], w_down, load_sem.at[2]),
    ]
    for load in loads:
        load.start()

    barrier = pltpu.get_barrier_semaphore()
    for d in range(1, 16):
        pl.semaphore_signal(barrier, inc=1, device_id={"expert": peer(e, d)}, device_id_type=MESH)
    pl.semaphore_signal(barrier, inc=1, device_id={"tensor": 1 - c}, device_id_type=MESH)

    eye = lax.broadcasted_iota(jnp.int32, (ROWS, ROWS), 0) == lax.broadcasted_iota(
        jnp.int32, (ROWS, ROWS), 1
    )
    ids = ids_ref[...]
    rw = rw_ref[...]
    for d in range(16):
        row = jnp.sum(jnp.where(ids == peer(e, d), rw, 0.0), axis=0, keepdims=True)
        wrow_out[d, :, 0:ROWS] = jnp.broadcast_to(row, (8, ROWS))
    tok[0, 0] = tok_ref[...]
    pl.semaphore_wait(barrier, 16)

    def send(src, dst, s_sem, r_sem, **where):
        return pltpu.make_async_remote_copy(
            src_ref=src, dst_ref=dst, send_sem=s_sem, recv_sem=r_sem,
            device_id=where, device_id_type=MESH,
        )

    tok_z = [
        send(tok_ref, tok.at[dz, 0], tok_send.at[dz, 0], tok_recv.at[dz, 0], expert=peer(e, 4 * dz))
        for dz in range(1, 4)
    ]
    tok_xy = [
        [
            send(
                tok.at[dz, 0] if dz else tok_ref, tok.at[dz, k], tok_send.at[dz, k],
                tok_recv.at[dz, k], expert=peer(e, k),
            )
            for k in (1, 2)
        ]
        for dz in range(4)
    ]
    near = 1 + c
    far = 2 - c
    near_dev = e + (1 - c) * (1 - 2 * (e % 2)) + c * (2 - 4 * ((e // 2) % 2))
    far_dev = e + c * (1 - 2 * (e % 2)) + (1 - c) * (2 - 4 * ((e // 2) % 2))
    tok_diag = [
        send(tok.at[dz, near], tok.at[dz, 3], tok_send.at[dz, 3], tok_recv.at[dz, 3], expert=far_dev)
        for dz in range(4)
    ]

    def wait_tok(k, dz):
        send(tok.at[dz, k], tok.at[dz, k], tok_send.at[0, 0], tok_recv.at[dz, k], expert=near_dev).wait_recv()

    for cp in tok_xy[0]:
        cp.start()
    for cp in tok_z:
        cp.start()
    rows_sent = [
        send(wrow_out.at[d], wrow_in.at[d], row_send.at[d], row_recv.at[d], expert=peer(e, d))
        for d in range(1, 16)
    ]

    wrow_in[0] = wrow_out[0]
    square = (half // 128, half // 128)
    diagonal = lax.broadcasted_iota(jnp.int32, square, 0) == lax.broadcasted_iota(jnp.int32, square, 1)
    for g, ref in ((0, gs_ref), (1, us_ref)):
        blocks = ref[0]
        for j in range(ff // 128):
            row = blocks[j : j + 1, :]
            column = jnp.sum(jnp.where(diagonal, row, 0.0), axis=1, keepdims=True)
            scale_in[g, 0 : half // 128, j * 128 : (j + 1) * 128] = jnp.broadcast_to(
                column, (half // 128, 128)
            )
    blocks = ds_ref[0]
    for j in range(half // 128):
        scale_down[:, j * 128 : (j + 1) * 128] = jnp.broadcast_to(blocks[:, j : j + 1], (ff // 128, 128))

    def dequant_in(g):
        loads[g].wait()

        @pl.loop(0, half // 128)
        def _(i):
            at = pl.ds(pl.multiple_of(i * 128, 128), 128)
            w_in[g, at, :] = (w_in[g, at, :].astype(jnp.float32) * scale_in[g, pl.ds(i, 1), :]).astype(jnp.bfloat16)

    def dequant_down():
        loads[2].wait()

        @pl.loop(0, ff // 128)
        def _(i):
            at = pl.ds(pl.multiple_of(i * 128, 128), 128)
            w_down[at, :] = (w_down[at, :].astype(jnp.float32) * scale_down[pl.ds(i, 1), :]).astype(jnp.bfloat16)

    def pass_on(dz):
        tok_z[dz - 1].wait_recv()
        for cp in tok_xy[dz]:
            cp.start()

    def pass_diag(dz):
        wait_tok(near, dz)
        tok_diag[dz].start()

    parts = [
        send(part_out.at[k], part_in.at[k], part_send.at[k], part_recv.at[k], tensor=1 - c)
        for k in range(4)
    ]

    def gate_up(k):
        wait_tok(far, k)
        tok_diag[k].wait_recv()
        x = tok[k].reshape(4 * ROWS, half)

        @pl.loop(0, 2 * ff // 256)
        def _(t):
            g = t // (ff // 256)
            at = pl.ds(pl.multiple_of((t % (ff // 256)) * 256, 256), 256)
            p = jnp.dot(x, w_in[g, :, at], preferred_element_type=jnp.float32)
            part_own[k % 2, g, :, at] = p
            part_out[k, g, :, at] = p.astype(jnp.bfloat16)

        parts[k].start()

    def down(k):
        parts[k].wait_recv()

        @pl.loop(0, ff // 256)
        def _(t):
            at = pl.ds(pl.multiple_of(t * 256, 256), 256)
            gate = part_own[k % 2, 0, :, at] + part_in[k, 0, :, at].astype(jnp.float32)
            up = part_own[k % 2, 1, :, at] + part_in[k, 1, :, at].astype(jnp.float32)
            hid[:, at] = (gate / (1.0 + jnp.exp(-gate)) * up).astype(jnp.bfloat16)

        columns = []
        for d in range(4):
            row = wrow_in[4 * k + d, 0:1, 0:ROWS]
            columns.append(jnp.sum(jnp.where(eye, row, 0.0), axis=1, keepdims=True))
        column = jnp.concatenate(columns, axis=0)
        h = hid[...]

        @pl.loop(0, half // 256)
        def _(t):
            at = pl.ds(pl.multiple_of(t * 256, 256), 256)
            y = jnp.dot(h, w_down[:, at], preferred_element_type=jnp.float32) * column
            part_y[k, :, :, at] = y.reshape(4, ROWS, 256).astype(jnp.bfloat16)

    diag_back = [
        send(part_y.at[dz, 3], diag_in.at[dz], y_send.at[0, dz], y_recv.at[0, dz], expert=near_dev)
        for dz in range(4)
    ]
    near_back = [
        send(part_y.at[dz, near], near_in.at[dz], y_send.at[1, dz], y_recv.at[1, dz], expert=near_dev)
        for dz in range(4)
    ]
    far_back = [
        send(part_y.at[dz, far], far_in.at[dz], y_send.at[2, dz], y_recv.at[2, dz], expert=far_dev)
        for dz in range(4)
    ]
    z_back = [
        send(col_out.at[dz], z_in.at[dz], z_send.at[dz], z_recv.at[dz], expert=peer(e, 4 * dz))
        for dz in range(1, 4)
    ]

    def back(dz):
        diag_back[dz].start()
        near_back[dz].start()

    def turn(dz):
        diag_back[dz].wait_recv()
        part_y[dz, far] = (
            part_y[dz, far].astype(jnp.float32) + diag_in[dz].astype(jnp.float32)
        ).astype(jnp.bfloat16)
        far_back[dz].start()

    def column_sum(dz):
        near_back[dz].wait_recv()
        far_back[dz].wait_recv()
        total = (
            part_y[dz, 0].astype(jnp.float32)
            + near_in[dz].astype(jnp.float32)
            + far_in[dz].astype(jnp.float32)
        )
        if dz:
            col_out[dz] = total.astype(jnp.bfloat16)
            z_back[dz - 1].start()
        else:
            acc[...] = total

    dequant_in(0)
    pass_diag(0)
    pass_on(1)
    for cp in rows_sent:
        cp.start()
    dequant_in(1)
    pass_on(2)
    gate_up(0)
    pass_diag(1)
    dequant_down()
    pass_on(3)
    gate_up(1)
    pass_diag(2)
    for cp in rows_sent:
        cp.wait_recv()
    down(0)
    back(0)
    gate_up(2)
    pass_diag(3)
    turn(0)
    down(1)
    back(1)
    gate_up(3)
    turn(1)
    down(2)
    back(2)
    column_sum(0)
    down(3)
    back(3)
    column_sum(1)
    turn(2)
    column_sum(2)
    turn(3)
    column_sum(3)
    for dz in range(1, 4):
        z_back[dz - 1].wait_recv()
        acc[...] += z_in[dz].astype(jnp.float32)
    out_ref[...] = acc[...].astype(jnp.bfloat16)

    for cp in (
        tok_z + rows_sent + parts + tok_diag + diag_back + near_back + far_back + z_back
        + [cp for pair in tok_xy for cp in pair]
    ):
        cp.wait_send()


def fused_local(
    tokens, expert_ids, route_weights, gate_q, up_q, down_q, gate_scale, up_scale, down_scale
):
    rows, half = tokens.shape
    ff = gate_q.shape[2]
    bf16, f32 = jnp.bfloat16, jnp.float32
    vmem = pl.BlockSpec(memory_space=pltpu.VMEM)
    hbm = pl.BlockSpec(memory_space=pl.ANY)
    dma = pltpu.SemaphoreType.DMA
    return pl.pallas_call(
        fused_kernel,
        out_shape=jax.ShapeDtypeStruct((rows, half), bf16),
        in_specs=[vmem] * 6 + [hbm] * 3,
        out_specs=vmem,
        scratch_shapes=[
            pltpu.VMEM((4, 4, rows, half), bf16),
            pltpu.VMEM((2, half, ff), bf16),
            pltpu.VMEM((ff, half), bf16),
            pltpu.VMEM((2, 16, ff), f32),
            pltpu.VMEM((ff // 128, half), f32),
            pltpu.VMEM((2, 2, 4 * rows, ff), f32),
            pltpu.VMEM((4, 2, 4 * rows, ff), bf16),
            pltpu.VMEM((4, 2, 4 * rows, ff), bf16),
            pltpu.VMEM((4 * rows, ff), bf16),
            pltpu.VMEM((4, 4, rows, half), bf16),
            pltpu.VMEM((4, rows, half), bf16),
            pltpu.VMEM((4, rows, half), bf16),
            pltpu.VMEM((4, rows, half), bf16),
            pltpu.VMEM((4, rows, half), bf16),
            pltpu.VMEM((4, rows, half), bf16),
            pltpu.VMEM((rows, half), f32),
            pltpu.VMEM((16, 8, 128), f32),
            pltpu.VMEM((16, 8, 128), f32),
            dma((3,)),
            dma((4, 4)),
            dma((4, 4)),
            dma((4,)),
            dma((4,)),
            dma((16,)),
            dma((16,)),
            dma((3, 4)),
            dma((3, 4)),
            dma((4,)),
            dma((4,)),
        ],
        compiler_params=pltpu.CompilerParams(
            collective_id=0, has_side_effects=True, vmem_limit_bytes=58 * 1024 * 1024
        ),
        cost_estimate=pl.CostEstimate(
            flops=2 * 16 * rows * half * ff * 3,
            bytes_accessed=3 * 2 * half * ff,
            transcendentals=16 * rows * ff,
        ),
    )(
        tokens, expert_ids.T, route_weights.T, gate_scale.swapaxes(1, 2), up_scale.swapaxes(1, 2),
        down_scale, gate_q, up_q, down_q,
    )


def solution(mesh):
    return jax.shard_map(
        fused_local if mesh.shape["expert"] == 16 and mesh.shape["tensor"] == 2 else exchange_local,
        mesh=mesh,
        in_specs=(
            P(("groups", "expert"), "tensor"),
            P(("groups", "expert"), None),
            P(("groups", "expert"), None),
            P("expert", "tensor", None),
            P("expert", "tensor", None),
            P("expert", None, "tensor"),
            P("expert", "tensor", None),
            P("expert", "tensor", None),
            P("expert", None, "tensor"),
        ),
        out_specs=P(("groups", "expert"), "tensor"),
        check_vma=False,
    )
```
